512 devices in a mesh: grid: 64 (over y, z), freq: 8 (over x, core).
Axes of the slice: x: 4, y: 4, z: 16, core: 2. Of those that a mesh axis runs over, the one named last changes fastest.
Arguments:
- bin_index: int32 [16], P('freq'), may hold values from 64 to 511
- microphones: float32 [3, 128], replicated, may hold values from -0.5 to 0.5
- grid_points: float32 [3, 262144], P(None, 'grid'), may hold values from -1 to 1
- cross_spectra: float32 [16, 2, 128, 128], P('freq'), may hold values from -1 to 3, as said below
- initial_strengths: float32 [262144], P('grid'), may hold values from 0.05 to 2
Outputs:
- strengths: float32 [262144], P('grid')
The draws below stay inside these ranges and needn't reach their ends.
Inputs may be any that keep to these rules, and one draw needn't show every extreme that they name: `cross_spectra`: for every bin the real part is symmetric and the imaginary part antisymmetric.
All inputs are finite; a program needn't handle non-finite values.
Results may differ from the reference program's by a relative error of at most 0.0045.
Values sent between devices are 32-bit elements; how exact they have to be, the bound alone decides.
A program may use at most 64 MiB of HBM per device.

```python
import math
import jax
import jax.numpy as jnp
from jax import lax

M = 128
SPECTRUM = 1024
ITERS = 2
POINTS = 262144
BINS = 16


LOG_TEN = 2.302585092994046


def draw_cross_spectra(key, part):
    key = jax.random.fold_in(key, 7)
    subkeys = jax.random.split(key, 3)
    matrix_shape = (BINS, M, M)
    first_draw = jax.random.normal(subkeys[0], matrix_shape, jnp.float32)
    second_draw = jax.random.normal(subkeys[1], matrix_shape, jnp.float32)
    levels = jax.random.uniform(subkeys[2], (BINS, M), jnp.float32, 0.0, 1.0)
    identity = jnp.eye(M, dtype=jnp.float32)
    symmetric = (first_draw + jnp.swapaxes(first_draw, 1, 2)) * (1.0 - identity)
    antisym = second_draw - jnp.swapaxes(second_draw, 1, 2)
    diagonal = 3.0 * jnp.exp(LOG_TEN * (levels / jnp.max(levels) - 1.0))
    real_part = 0.6 * symmetric / jnp.max(jnp.abs(symmetric)) + identity * diagonal[:, :, None]
    imag_part = antisym / jnp.max(jnp.abs(antisym))
    return jnp.stack([real_part, imag_part], axis=1)


def plant(result, rng, low, largest):
    longest = result.shape.index(max(result.shape))
    spots = []
    for shift in (0, 1):
        where = [jax.random.randint(jax.random.fold_in(rng, axis), (), 0, length) for axis, length in enumerate(result.shape)]
        where[longest] = (where[longest] + shift) % result.shape[longest]
        spots.append(tuple(where))
    return result.at[spots[0]].set(low).at[spots[1]].set(largest)


def steps_of(own_key, shape, pieces, smallest, top_value):
    level = 1.0
    for dim, parts in pieces:
        heights = jax.random.uniform(jax.random.fold_in(jax.random.fold_in(own_key, 6), dim), (parts,), jnp.float32, smallest / len(pieces), top_value / len(pieces))
        level = level * jnp.repeat(jnp.exp(heights), shape[dim] // parts).reshape((-1,) + (1,) * (len(shape) - 1 - dim))
    return level


def setup_inputs(seed: int = 0) -> dict:
    arg_keys = jax.random.split(jax.random.key(seed), 6)
    return {
        "bin_index": plant(jax.random.randint(arg_keys[0], (BINS,), SPECTRUM // 16, SPECTRUM // 2), jax.random.fold_in(arg_keys[0], 1), SPECTRUM // 16, (SPECTRUM // 2) - 1).astype(jnp.int32),
        "microphones": jnp.clip(jax.random.uniform(arg_keys[1], (3, M), jnp.float32, -0.5, 0.5), -0.5, 0.5),
        "grid_points": jnp.clip(jax.random.uniform(arg_keys[2], (3, POINTS), jnp.float32, -1.0, 1.0) * steps_of(arg_keys[2], (3, POINTS), ((1, 64),), -0.4, 0.0), -1.0, 1.0),
        "cross_spectra": draw_cross_spectra(jax.random.fold_in(arg_keys[5], 71), 0),
        "initial_strengths": jnp.clip(jnp.exp(math.log(2.0) - 3.6888794 * jax.random.uniform(arg_keys[4], (POINTS,), jnp.float32) ** steps_of(arg_keys[4], (POINTS,), ((0, 64),), -0.2, 0.2)), 0.05, 2.0),
    }


HEIGHT = 2.5
REFERENCE_RANGE = 2.5
WAVE_STEP = 2.0 * math.pi * 25.0 / 343.0

def steer_one(bin_one, microphones, grid_points):
    delta_x = grid_points[0][None, :] - microphones[0][:, None]
    delta_y = grid_points[1][None, :] - microphones[1][:, None]
    delta_z = grid_points[2][None, :] + HEIGHT - microphones[2][:, None]
    distance = jnp.sqrt(delta_x * delta_x + delta_y * delta_y + delta_z * delta_z)
    wavenumber = bin_one.astype(distance.dtype) * WAVE_STEP
    phase_angle = wavenumber * distance
    amplitude = REFERENCE_RANGE / distance
    return jnp.concatenate([amplitude * jnp.cos(phase_angle), -amplitude * jnp.sin(phase_angle)], axis=0).astype(jnp.bfloat16)

def cross_model(steering, weights, inverse):
    weighted = (steering.astype(jnp.float32) * weights[None, :]).astype(jnp.bfloat16)
    gram_rows = jnp.dot(weighted.astype(jnp.float32), steering.astype(jnp.float32).T, preferred_element_type=jnp.float32)
    real_part = gram_rows[:M, :M] + gram_rows[M:, M:]
    imag_part = gram_rows[M:, :M] - gram_rows[:M, M:]
    return (real_part * inverse, imag_part * inverse)

def reference(bin_index, microphones, grid_points, cross_spectra, initial_strengths):
    inverse = 1.0 / POINTS
    strengths = initial_strengths
    for iteration in range(ITERS):

        def model_pass(total, inputs):
            bin_one, cross_one = inputs
            steering = steer_one(bin_one, microphones, grid_points)
            model_real, model_imag = cross_model(steering, strengths, inverse)
            residual = (cross_one - jnp.stack([model_real, model_imag])).astype(jnp.bfloat16)
            operator = jnp.concatenate([jnp.concatenate([residual[0], -residual[1]], axis=1), jnp.concatenate([residual[1], residual[0]], axis=1)], axis=0)
            applied = jnp.dot(operator.astype(jnp.float32), steering.astype(jnp.float32), preferred_element_type=jnp.float32)
            return (total + lax.optimization_barrier(jnp.sum(steering.astype(jnp.float32) * applied, axis=0)), None)
        grad_sum, _ = lax.scan(model_pass, jnp.zeros((POINTS,), jnp.float32), (bin_index, cross_spectra))
        gradient = -2.0 * inverse * grad_sum
        grad_norm = jnp.sum(gradient * gradient)

        def direction_pass(total, bin_one):
            steering = steer_one(bin_one, microphones, grid_points)
            direction_real, direction_imag = cross_model(steering, gradient, inverse)
            return (total + jnp.sum(direction_real * direction_real + direction_imag * direction_imag), None)
        curvature, _ = lax.scan(direction_pass, jnp.zeros((), jnp.float32), bin_index)
        step_length = 0.5 * grad_norm / curvature
        strengths = jnp.maximum(strengths - step_length * gradient, 0.0)
    return strengths
```

```python
import functools
import math

import jax
import jax.numpy as jnp
from jax import lax
from jax.experimental import pallas as pl
from jax.experimental.pallas import tpu as pltpu
from jax.sharding import PartitionSpec as P

ITERS = 2
GRID_Y = 4

HEIGHT = 2.5
REFERENCE_RANGE = 2.5
TURN_STEP = 25.0 / 343.0
HALF_PI = math.pi / 2.0

MESH = pl.DeviceIdType.MESH
F32 = jnp.float32
BF16 = jnp.bfloat16

SIN_COEFFS = (3.141590270, -5.167406733, 2.544010518, -0.559462455)
COS_COEFFS = (0.999993249, -4.933934668, 4.041248102, -1.222031763)


def horner(coeffs, u):
    value = coeffs[-1]
    for c in coeffs[-2::-1]:
        value = value * u + c
    return value


def kernel(
    grid_size,
    freq_size,
    bins_ref,
    mics_ref,
    points_ref,
    cross_ref,
    start_ref,
    out_ref,
    mic_cols,
    steer,
    gram,
    strength,
    ysend,
    yrecv,
    zsend,
    zrecv,
    gather,
    grads,
    parts_a,
    parts_b,
    send_sem,
    recv_sem,
):
    nb = bins_ref.shape[0]
    mics = mics_ref.shape[1]
    points = points_ref.shape[1]
    ny = GRID_Y
    nz = grid_size // ny
    rows_y = mics // ny
    rows_z = nb * rows_y // nz
    total = points * grid_size
    inverse = 1.0 / total

    g = lax.axis_index("grid")
    f = lax.axis_index("freq")
    y, z = lax.div(g, nz), lax.rem(g, nz)

    def at(y_id, z_id, f_id):
        return {"grid": y_id * nz + z_id, "freq": f_id}

    z_ids = [lax.rem(z + d, nz) for d in range(1, nz)]
    y_ids = [lax.rem(y + d, ny) for d in range(1, ny)]
    f_ids = [lax.rem(f + d, freq_size) for d in range(1, freq_size)]
    z_peers = [at(y, i, f) for i in z_ids]
    y_peers = [at(i, z, f) for i in y_ids]
    f_peers = [at(y, z, i) for i in f_ids]
    fy_peers = y_peers + f_peers + [at(i, z, j) for i in y_ids for j in f_ids]

    barrier = pltpu.get_barrier_semaphore()
    for peer in z_peers + fy_peers:
        pl.semaphore_signal(barrier, inc=1, device_id=peer, device_id_type=MESH)

    def send(phase, src, dst, peer):
        pltpu.make_async_remote_copy(
            src_ref=src,
            dst_ref=dst,
            send_sem=send_sem.at[phase],
            recv_sem=recv_sem.at[phase],
            device_id=peer,
            device_id_type=MESH,
        ).start()

    def arrive(phase, like):
        pltpu.make_async_copy(like, like, recv_sem.at[phase]).wait()

    def sent(phase, like):
        pltpu.make_async_copy(like, like, send_sem.at[phase]).wait()

    for axis in range(3):
        mic_cols[axis] = jnp.transpose(jnp.broadcast_to(mics_ref[axis : axis + 1, :], (mics, mics)))
    scale = [bins_ref[b].astype(F32) * TURN_STEP for b in range(nb)]
    sub, lanes = 16, 256
    blocks_m = mics // sub

    def steer_block(i, carry):
        m0 = pl.multiple_of(lax.rem(i, blocks_m) * sub, sub)
        c0 = pl.multiple_of(lax.div(i, blocks_m) * lanes, lanes)
        cols = pl.ds(c0, lanes)

        def mic(axis):
            tile = mic_cols[axis, pl.ds(m0, sub), :]
            return jnp.concatenate([tile] * (lanes // mics), axis=1)

        dx = points_ref[0:1, cols] - mic(0)
        dy = points_ref[1:2, cols] - mic(1)
        dz = (points_ref[2:3, cols] + HEIGHT) - mic(2)
        square = dx * dx + dy * dy + dz * dz
        inv = lax.rsqrt(square)
        inv = inv * (1.5 - 0.5 * square * inv * inv)
        distance = square * inv
        amplitude = REFERENCE_RANGE * inv
        for b in range(nb):
            turns = distance * scale[b]
            frac = turns - jnp.round(turns)
            u = frac * frac
            half_sin = frac * horner(SIN_COEFFS, u)
            half_cos = horner(COS_COEFFS, u)
            twice = (2.0 * amplitude) * half_sin
            real = amplitude - twice * half_sin
            imag = -(twice * half_cos)
            steer[b, pl.ds(m0, sub), cols] = real.astype(BF16)
            steer[b, pl.ds(m0 + mics, sub), cols] = imag.astype(BF16)
        return carry

    lax.fori_loop(0, blocks_m * (points // lanes), steer_block, 0)

    strength[...] = start_ref[...]

    row = lax.broadcasted_iota(jnp.int32, (mics, mics), 0)
    col = lax.broadcasted_iota(jnp.int32, (mics, mics), 1)
    upper = row <= col
    diagonal = row == col

    chunk = 1024

    def gram_into(weights_of):
        gram[...] = jnp.zeros_like(gram)

        def step(k, carry):
            cols = pl.ds(pl.multiple_of(k * chunk, chunk), chunk)
            w = weights_of(cols)
            for b in range(nb):
                s = steer[b, :, cols]
                weighted = (s.astype(F32) * w).astype(BF16)
                gram[b] += lax.dot_general(
                    weighted, s, (((1,), (1,)), ((), ())), preferred_element_type=F32
                )
            return carry

        lax.fori_loop(0, points // chunk, step, 0)

    def packed(b):
        real = gram[b, :mics, :mics] + gram[b, mics:, mics:]
        imag = gram[b, mics:, :mics] - gram[b, :mics, mics:]
        return jnp.where(upper, real, imag)

    def reduce_scatter(it, which):
        slot = 2 * it + which
        phase = 8 * it + 4 * which
        for b in range(nb):
            full = packed(b)
            for j in range(ny):
                ysend[slot, j, b] = full[j * rows_y : (j + 1) * rows_y, :]
        for d, peer in enumerate(y_peers):
            send(phase, ysend.at[slot, y_ids[d]], yrecv.at[slot, d], peer)
        arrive(phase, yrecv.at[slot])
        part = ysend[slot, y]
        for d in range(ny - 1):
            part = part + yrecv[slot, d]
        zsend[slot] = part.reshape(nz, rows_z, mics)
        for d, peer in enumerate(z_peers):
            send(phase + 1, zsend.at[slot, z_ids[d]], zrecv.at[slot, d], peer)
        arrive(phase + 1, zrecv.at[slot])
        mine = zsend[slot, z]
        for d in range(nz - 1):
            mine = mine + zrecv[slot, d]
        return mine

    for it in range(ITERS):
        gram_into(lambda cols: strength[:, cols])
        if it == 0:
            pl.semaphore_wait(barrier, len(z_peers) + len(fy_peers))
        mine = reduce_scatter(it, 0)
        gather[it, y, z] = mine
        for peer in z_peers:
            send(8 * it + 2, gather.at[it, y, z], gather.at[it, y, z], peer)
        arrive(8 * it + 2, gather.at[it, 0, pl.ds(0, nz - 1)])
        for peer in y_peers:
            send(8 * it + 3, gather.at[it, y], gather.at[it, y], peer)
        arrive(8 * it + 3, gather.at[it, pl.ds(0, ny - 1)])
        operators = []
        for b in range(nb):
            model = jnp.concatenate(
                [gather[it, j].reshape(nb, rows_y, mics)[b] for j in range(ny)], axis=0
            )
            flipped = jnp.transpose(model)
            model_real = jnp.where(upper, model, flipped)
            model_imag = jnp.where(diagonal, 0.0, jnp.where(upper, -flipped, model))
            res_real = cross_ref[b, 0] - model_real * inverse
            res_imag = cross_ref[b, 1] - model_imag * inverse
            operators.append(
                jnp.concatenate(
                    [
                        jnp.concatenate([res_real, -res_imag], axis=1),
                        jnp.concatenate([res_imag, res_real], axis=1),
                    ],
                    axis=0,
                ).astype(BF16)
            )

        width = 512
        for k in range(points // width):
            cols = pl.ds(k * width, width)
            term = None
            for b in range(nb):
                s = steer[b, :, cols]
                applied = jnp.dot(operators[b], s, preferred_element_type=F32)
                product = (s.astype(F32) * applied).reshape(2 * mics // 8, 8, width)
                product = jnp.sum(product, axis=0)
                term = product if term is None else term + product
            grads[it, f, :, cols] = jnp.sum(term, axis=0, keepdims=True)
        for peer in f_peers:
            send(16 + it, grads.at[it, f], grads.at[it, f], peer)
        arrive(16 + it, grads.at[it, pl.ds(0, freq_size - 1)])
        gradient = grads[it, 0]
        for j in range(1, freq_size):
            gradient = gradient + grads[it, j]
        gradient = (-2.0 * inverse) * gradient
        grads[it, freq_size] = gradient

        gram_into(lambda cols: grads[it, freq_size, :, cols])
        mine = reduce_scatter(it, 1) * inverse
        index = lax.broadcasted_iota(jnp.int32, (rows_z, mics), 0) + z * rows_z
        index = lax.rem(index, rows_y) + y * rows_y
        column = lax.broadcasted_iota(jnp.int32, (rows_z, mics), 1)
        curved = jnp.sum(mine * mine * jnp.where(index == column, 1.0, 2.0), axis=0, keepdims=True)
        squares = gradient * gradient
        normed = squares[:, :mics]
        for k in range(1, points // mics):
            normed = normed + squares[:, k * mics : (k + 1) * mics]
        own = y * freq_size + f
        parts_a[it, own] = jnp.concatenate([normed * (1.0 / freq_size), curved], axis=0)
        for peer in fy_peers:
            send(18 + 2 * it, parts_a.at[it, own], parts_a.at[it, own], peer)
        arrive(18 + 2 * it, parts_a.at[it, pl.ds(0, ny * freq_size - 1)])
        parts_b[it, z] = jnp.sum(parts_a[it], axis=0)
        for peer in z_peers:
            send(19 + 2 * it, parts_b.at[it, z], parts_b.at[it, z], peer)
        arrive(19 + 2 * it, parts_b.at[it, pl.ds(0, nz - 1)])
        sums = jnp.sum(jnp.sum(parts_b[it], axis=0), axis=1, keepdims=True)
        step_length = 0.5 * sums[0:1] / sums[1:2]
        updated = jnp.maximum(strength[...] - step_length * gradient, 0.0)
        if it < ITERS - 1:
            strength[...] = updated
        else:
            out_ref[...] = updated

    for it in range(ITERS):
        for which in range(2):
            slot, phase = 2 * it + which, 8 * it + 4 * which
            sent(phase, yrecv.at[slot])
            sent(phase + 1, zrecv.at[slot])
        sent(8 * it + 2, gather.at[it, 0, pl.ds(0, nz - 1)])
        sent(8 * it + 3, gather.at[it, pl.ds(0, ny - 1)])
        sent(16 + it, grads.at[it, pl.ds(0, freq_size - 1)])
        sent(18 + 2 * it, parts_a.at[it, pl.ds(0, ny * freq_size - 1)])
        sent(19 + 2 * it, parts_b.at[it, pl.ds(0, nz - 1)])


def local(grid_size, freq_size, bin_index, microphones, grid_points, cross_spectra, initial_strengths):
    nb = bin_index.shape[0]
    mics = microphones.shape[1]
    points = grid_points.shape[1]
    ny = GRID_Y
    nz = grid_size // ny
    rows_y = mics // ny
    rows_z = nb * rows_y // nz
    vmem = pl.BlockSpec(memory_space=pltpu.VMEM)
    out = pl.pallas_call(
        functools.partial(kernel, grid_size, freq_size),
        out_shape=jax.ShapeDtypeStruct((1, points), F32),
        in_specs=[pl.BlockSpec(memory_space=pltpu.SMEM), vmem, vmem, vmem, vmem],
        out_specs=vmem,
        scratch_shapes=[
            pltpu.VMEM((3, mics, mics), F32),
            pltpu.VMEM((nb, 2 * mics, points), BF16),
            pltpu.VMEM((nb, 2 * mics, 2 * mics), F32),
            pltpu.VMEM((1, points), F32),
            pltpu.VMEM((2 * ITERS, ny, nb, rows_y, mics), F32),
            pltpu.VMEM((2 * ITERS, ny - 1, nb, rows_y, mics), F32),
            pltpu.VMEM((2 * ITERS, nz, rows_z, mics), F32),
            pltpu.VMEM((2 * ITERS, nz - 1, rows_z, mics), F32),
            pltpu.VMEM((ITERS, ny, nz, rows_z, mics), F32),
            pltpu.VMEM((ITERS, freq_size + 1, 1, points), F32),
            pltpu.VMEM((ITERS, ny * freq_size, 2, mics), F32),
            pltpu.VMEM((ITERS, nz, 2, mics), F32),
            pltpu.SemaphoreType.DMA((22,)),
            pltpu.SemaphoreType.DMA((22,)),
        ],
        compiler_params=pltpu.CompilerParams(
            collective_id=0, has_side_effects=True, vmem_limit_bytes=40 * 1024 * 1024
        ),
        name="map_fit",
    )(bin_index, microphones, grid_points, cross_spectra, initial_strengths.reshape(1, points))
    return out.reshape(points)


def solution(mesh):
    placed = (P("freq"), P(), P(None, "grid"), P("freq", None, None, None), P("grid"))
    body = functools.partial(local, mesh.shape["grid"], mesh.shape["freq"])
    return jax.shard_map(body, mesh=mesh, in_specs=placed, out_specs=P("grid"), check_vma=False)
```

```python
import functools
import math

import jax
import jax.numpy as jnp
from jax import lax
from jax.experimental import pallas as pl
from jax.experimental.pallas import tpu as pltpu
from jax.sharding import PartitionSpec as P

ITERS = 2
GRID_Y = 4
NEAR = 4

HEIGHT = 2.5
REFERENCE_RANGE = 2.5
TURN_STEP = 25.0 / 343.0
HALF_PI = math.pi / 2.0

MESH = pl.DeviceIdType.MESH
F32 = jnp.float32
BF16 = jnp.bfloat16

SIN_COEFFS = (3.141590270, -5.167406733, 2.544010518, -0.559462455)
COS_COEFFS = (0.999993249, -4.933934668, 4.041248102, -1.222031763)


def horner(coeffs, u):
    value = coeffs[-1]
    for c in coeffs[-2::-1]:
        value = value * u + c
    return value


def kernel(
    grid_size,
    freq_size,
    bins_hbm,
    mics_hbm,
    points_hbm,
    cross_hbm,
    start_hbm,
    out_ref,
    bins_ref,
    mics_ref,
    points_ref,
    cross_ref,
    strength,
    mic_cols,
    steer,
    gram,
    scattered,
    arrived,
    far,
    gather,
    grads,
    norms,
    parts_a,
    parts_b,
    load_sem,
    send_sem,
    recv_sem,
):
    nb = bins_ref.shape[0]
    mics = mics_ref.shape[1]
    points = points_ref.shape[1]
    ny = GRID_Y
    nz = grid_size // ny
    far_size = nz // NEAR
    chunks = ny * NEAR
    rows = mics // chunks
    total = points * grid_size
    inverse = 1.0 / total

    g = lax.axis_index("grid")
    f = lax.axis_index("freq")
    y, z = lax.div(g, nz), lax.rem(g, nz)
    chunk_id = y * NEAR + lax.rem(z, NEAR)
    far_id = lax.div(z, NEAR)

    def at(y_id, z_id, f_id):
        return {"grid": y_id * nz + z_id, "freq": f_id}

    def near(reach):
        peers = []
        for dy in range(ny):
            y_id = lax.rem(y + dy, ny)
            for dz in reach:
                if dy == 0 and isinstance(dz, int) and dz == 0:
                    continue
                z_id = lax.rem(z + dz + nz, nz)
                peers.append((y_id * NEAR + lax.rem(z_id, NEAR), at(y_id, z_id, f)))
        return peers

    two = 2 - 4 * lax.rem(f, 2)
    owners = near((0, 1, -1, two))
    clients = near((0, 1, -1, -two))
    neighbours = near((0, 1, -1, 2, -2))
    far_peers = [at(y, lax.rem(z + d * NEAR, nz), f) for d in range(1, far_size)]
    f_peers = [at(y, z, lax.rem(f + d, freq_size)) for d in range(1, freq_size)]

    loads = [
        pltpu.make_async_copy(src, dst, load_sem.at[i])
        for i, (src, dst) in enumerate(
            (
                (bins_hbm, bins_ref),
                (mics_hbm, mics_ref),
                (points_hbm, points_ref),
                (start_hbm, strength),
                (cross_hbm, cross_ref),
            )
        )
    ]
    for load in loads:
        load.start()

    greeted = [peer for _, peer in neighbours] + far_peers + f_peers
    barrier = pltpu.get_barrier_semaphore()
    for peer in greeted:
        pl.semaphore_signal(barrier, inc=1, device_id=peer, device_id_type=MESH)

    unsent = []

    def begin(phase, copies, like):
        for src, dst, peer in copies:
            pltpu.make_async_remote_copy(
                src_ref=src,
                dst_ref=dst,
                send_sem=send_sem.at[phase],
                recv_sem=recv_sem.at[phase],
                device_id=peer,
                device_id_type=MESH,
            ).start()
        if copies:
            unsent.append((phase, like))

    def finish(phase, copies, like):
        if copies:
            pltpu.make_async_copy(like, like, recv_sem.at[phase]).wait()

    def exchange(phase, copies, like):
        begin(phase, copies, like)
        finish(phase, copies, like)

    for load in loads[:3]:
        load.wait()

    for axis in range(3):
        mic_cols[axis] = jnp.transpose(jnp.broadcast_to(mics_ref[axis : axis + 1, :], (mics, mics)))
    scale = [bins_ref[b].astype(F32) * TURN_STEP for b in range(nb)]
    sub, lanes = 16, 512
    blocks_m = mics // sub

    def steer_block(i, carry):
        m0 = pl.multiple_of(lax.rem(i, blocks_m) * sub, sub)
        c0 = pl.multiple_of(lax.div(i, blocks_m) * lanes, lanes)
        cols = pl.ds(c0, lanes)

        def mic(axis):
            tile = mic_cols[axis, pl.ds(m0, sub), :]
            return jnp.concatenate([tile] * (lanes // mics), axis=1)

        dx = points_ref[0:1, cols] - mic(0)
        dy = points_ref[1:2, cols] - mic(1)
        dz = (points_ref[2:3, cols] + HEIGHT) - mic(2)
        square = dx * dx + dy * dy + dz * dz
        inv = lax.rsqrt(square)
        inv = inv * (1.5 - 0.5 * square * inv * inv)
        distance = square * inv
        amplitude = REFERENCE_RANGE * inv
        for b in range(nb):
            turns = distance * scale[b]
            frac = turns - jnp.round(turns)
            u = frac * frac
            half_sin = frac * horner(SIN_COEFFS, u)
            half_cos = horner(COS_COEFFS, u)
            twice = (2.0 * amplitude) * half_sin
            real = amplitude - twice * half_sin
            imag = -(twice * half_cos)
            steer[b, pl.ds(m0, sub), cols] = real.astype(BF16)
            steer[b, pl.ds(m0 + mics, sub), cols] = imag.astype(BF16)
        return carry

    lax.fori_loop(0, blocks_m * (points // lanes), steer_block, 0)

    row = lax.broadcasted_iota(jnp.int32, (mics, mics), 0)
    col = lax.broadcasted_iota(jnp.int32, (mics, mics), 1)
    upper = row <= col
    diagonal = row == col

    def gram_of(b, weights):
        s = steer[b]
        gram[b] = lax.dot_general(
            (s.astype(F32) * weights).astype(BF16),
            s,
            (((1,), (1,)), ((), ())),
            preferred_element_type=F32,
        )
        real = gram[b, :mics, :mics] + gram[b, mics:, mics:]
        imag = gram[b, mics:, :mics] - gram[b, :mics, mics:]
        return jnp.where(upper, real, imag)

    def summed(slot, phase, weights):
        for b in range(nb):
            scattered[slot, :, b] = gram_of(b, weights).reshape(chunks, rows, mics)
        if slot == 0:
            pl.semaphore_wait(barrier, len(greeted))
        exchange(
            phase,
            [
                (scattered.at[slot, k], arrived.at[slot, i], peer)
                for i, (k, peer) in enumerate(owners)
            ],
            arrived.at[slot],
        )
        far[slot, far_id] = scattered[slot, chunk_id] + jnp.sum(arrived[slot], axis=0)
        exchange(
            phase + 1,
            [(far.at[slot, far_id], far.at[slot, far_id], peer) for peer in far_peers],
            far.at[slot, pl.ds(0, far_size - 1)],
        )
        return jnp.sum(far[slot], axis=0)

    for it in range(ITERS):
        base = 9 * it

        if it == 0:
            loads[3].wait()
        gather[it, chunk_id] = summed(2 * it, base, strength[...])
        exchange(
            base + 2,
            [(gather.at[it, chunk_id], gather.at[it, chunk_id], peer) for _, peer in clients],
            gather.at[it, pl.ds(0, chunks - 1)],
        )
        if it == 0:
            loads[4].wait()
        operators = []
        for b in range(nb):
            model = gather[it, :, b].reshape(mics, mics)
            flipped = jnp.transpose(model)
            model_real = jnp.where(upper, model, flipped)
            model_imag = jnp.where(diagonal, 0.0, jnp.where(upper, -flipped, model))
            res_real = cross_ref[b, 0] - model_real * inverse
            res_imag = cross_ref[b, 1] - model_imag * inverse
            operators.append(
                jnp.concatenate(
                    [
                        jnp.concatenate([res_real, -res_imag], axis=1),
                        jnp.concatenate([res_imag, res_real], axis=1),
                    ],
                    axis=0,
                ).astype(BF16)
            )

        width = 512
        for k in range(points // width):
            cols = pl.ds(k * width, width)
            term = None
            for b in range(nb):
                s = steer[b, :, cols]
                applied = jnp.dot(operators[b], s, preferred_element_type=F32)
                product = (s.astype(F32) * applied).reshape(2 * mics // 8, 8, width)
                product = jnp.sum(product, axis=0)
                term = product if term is None else term + product
            grads[it, f, :, cols] = jnp.sum(term, axis=0, keepdims=True)
        exchange(
            base + 3,
            [(grads.at[it, f], grads.at[it, f], peer) for peer in f_peers],
            grads.at[it, pl.ds(0, freq_size - 1)],
        )
        gradient = grads[it, 0]
        for j in range(1, freq_size):
            gradient = gradient + grads[it, j]
        gradient = (-2.0 * inverse) * gradient
        squares = gradient * gradient
        normed = squares[:, :mics]
        for k in range(1, points // mics):
            normed = normed + squares[:, k * mics : (k + 1) * mics]
        norms[it, far_id] = normed * (1.0 / freq_size)
        norm_copies = [(norms.at[it, far_id], norms.at[it, far_id], peer) for peer in far_peers]
        norm_like = norms.at[it, pl.ds(0, far_size - 1)]
        begin(base + 4, norm_copies, norm_like)

        mine = summed(2 * it + 1, base + 5, gradient) * inverse
        index = lax.broadcasted_iota(jnp.int32, (nb, rows, mics), 1) + chunk_id * rows
        column = lax.broadcasted_iota(jnp.int32, (nb, rows, mics), 2)
        curved = mine * mine * jnp.where(index == column, 1.0, 2.0)
        curved = jnp.sum(jnp.sum(curved, axis=0), axis=0, keepdims=True)
        finish(base + 4, norm_copies, norm_like)
        parts_a[it, f] = jnp.concatenate([jnp.sum(norms[it], axis=0), curved], axis=0)
        exchange(
            base + 7,
            [(parts_a.at[it, f], parts_a.at[it, f], peer) for peer in f_peers],
            parts_a.at[it, pl.ds(0, freq_size - 1)],
        )
        parts_b[it, chunk_id] = jnp.sum(parts_a[it], axis=0)
        exchange(
            base + 8,
            [(parts_b.at[it, chunk_id], parts_b.at[it, chunk_id], peer) for _, peer in clients],
            parts_b.at[it, pl.ds(0, chunks - 1)],
        )
        sums = jnp.sum(jnp.sum(parts_b[it], axis=0), axis=1, keepdims=True)
        step_length = 0.5 * sums[0:1] / sums[1:2]
        updated = jnp.maximum(strength[...] - step_length * gradient, 0.0)
        if it < ITERS - 1:
            strength[...] = updated
        else:
            out_ref[...] = updated

    for phase, like in unsent:
        pltpu.make_async_copy(like, like, send_sem.at[phase]).wait()


def local(grid_size, freq_size, bin_index, microphones, grid_points, cross_spectra, initial_strengths):
    nb = bin_index.shape[0]
    mics = microphones.shape[1]
    points = grid_points.shape[1]
    ny = GRID_Y
    nz = grid_size // ny
    far_size = nz // NEAR
    chunks = ny * NEAR
    rows = mics // chunks
    hbm = pl.BlockSpec(memory_space=pltpu.HBM)
    out = pl.pallas_call(
        functools.partial(kernel, grid_size, freq_size),
        out_shape=jax.ShapeDtypeStruct((1, points), F32),
        in_specs=[hbm] * 5,
        out_specs=pl.BlockSpec(memory_space=pltpu.VMEM),
        scratch_shapes=[
            pltpu.SMEM((nb,), jnp.int32),
            pltpu.VMEM((3, mics), F32),
            pltpu.VMEM((3, points), F32),
            pltpu.VMEM((nb, 2, mics, mics), F32),
            pltpu.VMEM((1, points), F32),
            pltpu.VMEM((3, mics, mics), F32),
            pltpu.VMEM((nb, 2 * mics, points), BF16),
            pltpu.VMEM((nb, 2 * mics, 2 * mics), F32),
            pltpu.VMEM((2 * ITERS, chunks, nb, rows, mics), F32),
            pltpu.VMEM((2 * ITERS, chunks - 1, nb, rows, mics), F32),
            pltpu.VMEM((2 * ITERS, far_size, nb, rows, mics), F32),
            pltpu.VMEM((ITERS, chunks, nb, rows, mics), F32),
            pltpu.VMEM((ITERS, freq_size, 1, points), F32),
            pltpu.VMEM((ITERS, far_size, 1, mics), F32),
            pltpu.VMEM((ITERS, freq_size, 2, mics), F32),
            pltpu.VMEM((ITERS, chunks, 2, mics), F32),
            pltpu.SemaphoreType.DMA((5,)),
            pltpu.SemaphoreType.DMA((9 * ITERS,)),
            pltpu.SemaphoreType.DMA((9 * ITERS,)),
        ],
        compiler_params=pltpu.CompilerParams(
            collective_id=0, has_side_effects=True, vmem_limit_bytes=48 * 1024 * 1024
        ),
        name="map_fit",
    )(bin_index, microphones, grid_points, cross_spectra, initial_strengths.reshape(1, points))
    return out.reshape(points)


def solution(mesh):
    placed = (P("freq"), P(), P(None, "grid"), P("freq", None, None, None), P("grid"))
    body = functools.partial(local, mesh.shape["grid"], mesh.shape["freq"])
    return jax.shard_map(body, mesh=mesh, in_specs=placed, out_specs=P("grid"), check_vma=False)
```

```python
import functools
import math

import jax
import jax.numpy as jnp
from jax import lax
from jax.experimental import pallas as pl
from jax.experimental.pallas import tpu as pltpu
from jax.sharding import PartitionSpec as P

ITERS = 2
GRID_Y = 4
CORES = 2
NEAR = 4

HEIGHT = 2.5
REFERENCE_RANGE = 2.5
TURN_STEP = 25.0 / 343.0
HALF_PI = math.pi / 2.0

MESH = pl.DeviceIdType.MESH
F32 = jnp.float32
BF16 = jnp.bfloat16

SIN_COEFFS = (3.141590270, -5.167406733, 2.544010518, -0.559462455)
COS_COEFFS = (0.999993249, -4.933934668, 4.041248102, -1.222031763)


def horner(coeffs, u):
    value = coeffs[-1]
    for c in coeffs[-2::-1]:
        value = value * u + c
    return value


def kernel(
    grid_size,
    freq_size,
    bins_hbm,
    mics_hbm,
    points_hbm,
    cross_hbm,
    start_hbm,
    out_ref,
    bins_ref,
    mics_ref,
    points_ref,
    cross_ref,
    strength,
    mic_cols,
    steer,
    gram,
    scattered,
    arrived,
    far,
    gather,
    grads,
    norms,
    parts_a,
    parts_b,
    load_sem,
    send_sem,
    recv_sem,
):
    nb = bins_ref.shape[0]
    mics = mics_ref.shape[1]
    points = points_ref.shape[1]
    ny = GRID_Y
    nz = grid_size // ny
    far_size = nz // NEAR
    chunks = ny * NEAR
    rows = mics // chunks
    total = points * grid_size
    inverse = 1.0 / total

    g = lax.axis_index("grid")
    f = lax.axis_index("freq")
    y, z = lax.div(g, nz), lax.rem(g, nz)
    cols_x = freq_size // CORES
    x, core = lax.div(f, CORES), lax.rem(f, CORES)
    chunk_id = y * NEAR + lax.rem(z, NEAR)
    far_id = lax.div(z, NEAR)

    def at(y_id, z_id, f_id):
        return {"grid": y_id * nz + z_id, "freq": f_id}

    def near(reach, x_reach=(0,)):
        steps = [
            (min(dx, cols_x - dx) + min(dy, ny - dy) + hops, dx, dy, dz)
            for dx in x_reach
            for dy in range(ny)
            for hops, dz in reach
        ]
        peers = []
        for hops, dx, dy, dz in sorted(steps, key=lambda step: -step[0]):
            if hops == 0:
                continue
            y_id = lax.rem(y + dy, ny)
            z_id = lax.rem(z + dz + nz, nz)
            f_id = lax.rem(x + dx, cols_x) * CORES + core
            peers.append((y_id * NEAR + lax.rem(z_id, NEAR), at(y_id, z_id, f_id)))
        return peers

    two = 2 - 4 * core
    owners = near(((0, 0), (1, 1), (1, -1), (2, two)))
    clients = near(((0, 0), (1, 1), (1, -1), (2, -two)))
    all_x = tuple(range(1, cols_x))
    clients_x = near(((0, 0), (1, 1), (1, -1), (2, -two)), (0,) + all_x)
    owners_x = near(((0, 0), (1, 1), (1, -1), (2, two)), all_x)
    neighbours = near(((0, 0), (1, 1), (1, -1), (2, 2), (2, -2)))
    far_peers = [at(y, lax.rem(z + d * NEAR, nz), f) for d in (2, 1, 3) if d < far_size]
    other_core = at(y, z, x * CORES + 1 - core)
    f_steps = [(dx, dc) for dx in (2, 1, 3) if dx < cols_x for dc in (1, 0)] + [(0, 1)]
    f_peers = [
        at(y, z, lax.rem(x + dx, cols_x) * CORES + lax.rem(core + dc, CORES)) for dx, dc in f_steps
    ]

    loads = [
        pltpu.make_async_copy(src, dst, load_sem.at[i])
        for i, (src, dst) in enumerate(
            (
                (bins_hbm, bins_ref),
                (mics_hbm, mics_ref),
                (points_hbm, points_ref),
                (start_hbm, strength),
                (cross_hbm, cross_ref),
            )
        )
    ]
    for load in loads:
        load.start()

    greeted = [peer for _, peer in neighbours] + far_peers + f_peers + [peer for _, peer in owners_x]
    barrier = pltpu.get_barrier_semaphore()
    for peer in greeted:
        pl.semaphore_signal(barrier, inc=1, device_id=peer, device_id_type=MESH)

    unsent = []

    def begin(phase, copies, like):
        for src, dst, peer in copies:
            pltpu.make_async_remote_copy(
                src_ref=src,
                dst_ref=dst,
                send_sem=send_sem.at[phase],
                recv_sem=recv_sem.at[phase],
                device_id=peer,
                device_id_type=MESH,
            ).start()
        if copies:
            unsent.append((phase, like))

    def finish(phase, copies, like):
        if copies:
            pltpu.make_async_copy(like, like, recv_sem.at[phase]).wait()

    def exchange(phase, copies, like):
        begin(phase, copies, like)
        finish(phase, copies, like)

    for load in loads[:3]:
        load.wait()

    for axis in range(3):
        mic_cols[axis] = jnp.transpose(jnp.broadcast_to(mics_ref[axis : axis + 1, :], (mics, mics)))
    scale = [bins_ref[b].astype(F32) * TURN_STEP for b in range(nb)]
    sub, lanes = 16, 512
    blocks_m = mics // sub

    def steer_block(i, carry):
        m0 = pl.multiple_of(lax.rem(i, blocks_m) * sub, sub)
        c0 = pl.multiple_of(lax.div(i, blocks_m) * lanes, lanes)
        cols = pl.ds(c0, lanes)

        def mic(axis):
            tile = mic_cols[axis, pl.ds(m0, sub), :]
            return jnp.concatenate([tile] * (lanes // mics), axis=1)

        dx = points_ref[0:1, cols] - mic(0)
        dy = points_ref[1:2, cols] - mic(1)
        dz = (points_ref[2:3, cols] + HEIGHT) - mic(2)
        square = dx * dx + dy * dy + dz * dz
        inv = lax.rsqrt(square)
        inv = inv * (1.5 - 0.5 * square * inv * inv)
        distance = square * inv
        amplitude = REFERENCE_RANGE * inv
        for b in range(nb):
            turns = distance * scale[b]
            frac = turns - jnp.round(turns)
            u = frac * frac
            half_sin = frac * horner(SIN_COEFFS, u)
            half_cos = horner(COS_COEFFS, u)
            twice = (2.0 * amplitude) * half_sin
            real = amplitude - twice * half_sin
            imag = -(twice * half_cos)
            steer[b, pl.ds(m0, sub), cols] = real.astype(BF16)
            steer[b, pl.ds(m0 + mics, sub), cols] = imag.astype(BF16)
        return carry

    lax.fori_loop(0, blocks_m * (points // lanes), steer_block, 0)

    row = lax.broadcasted_iota(jnp.int32, (mics, mics), 0)
    col = lax.broadcasted_iota(jnp.int32, (mics, mics), 1)
    upper = row <= col
    diagonal = row == col

    def gram_of(b, weights):
        s = steer[b]
        gram[b] = lax.dot_general(
            (s.astype(F32) * weights).astype(BF16),
            s,
            (((1,), (1,)), ((), ())),
            preferred_element_type=F32,
        )
        real = gram[b, :mics, :mics] + gram[b, mics:, mics:]
        imag = gram[b, mics:, :mics] - gram[b, :mics, mics:]
        return jnp.where(upper, real, imag)

    def summed(slot, phase, weights):
        for b in range(nb):
            scattered[slot, :, b] = gram_of(b, weights).reshape(chunks, rows, mics)
        if slot == 0:
            pl.semaphore_wait(barrier, len(greeted))
        exchange(
            phase,
            [
                (scattered.at[slot, k], arrived.at[slot, i], peer)
                for i, (k, peer) in enumerate(owners)
            ],
            arrived.at[slot],
        )
        far[slot, far_id] = scattered[slot, chunk_id] + jnp.sum(arrived[slot], axis=0)
        exchange(
            phase + 1,
            [(far.at[slot, far_id], far.at[slot, far_id], peer) for peer in far_peers],
            far.at[slot, pl.ds(0, far_size - 1)],
        )
        return jnp.sum(far[slot], axis=0)

    for it in range(ITERS):
        base = 9 * it

        if it == 0:
            loads[3].wait()
        gather[it, chunk_id] = summed(2 * it, base, strength[...])
        exchange(
            base + 2,
            [(gather.at[it, chunk_id], gather.at[it, chunk_id], peer) for _, peer in clients],
            gather.at[it, pl.ds(0, chunks - 1)],
        )
        if it == 0:
            loads[4].wait()
        operators = []
        for b in range(nb):
            model = gather[it, :, b].reshape(mics, mics)
            flipped = jnp.transpose(model)
            model_real = jnp.where(upper, model, flipped)
            model_imag = jnp.where(diagonal, 0.0, jnp.where(upper, -flipped, model))
            res_real = cross_ref[b, 0] - model_real * inverse
            res_imag = cross_ref[b, 1] - model_imag * inverse
            operators.append(
                jnp.concatenate(
                    [
                        jnp.concatenate([res_real, -res_imag], axis=1),
                        jnp.concatenate([res_imag, res_real], axis=1),
                    ],
                    axis=0,
                ).astype(BF16)
            )

        width = 512
        for k in range(points // width):
            cols = pl.ds(k * width, width)
            term = None
            for b in range(nb):
                s = steer[b, :, cols]
                applied = jnp.dot(operators[b], s, preferred_element_type=F32)
                product = (s.astype(F32) * applied).reshape(2 * mics // 8, 8, width)
                product = jnp.sum(product, axis=0)
                term = product if term is None else term + product
            grads[it, f, :, cols] = jnp.sum(term, axis=0, keepdims=True)
        exchange(
            base + 3,
            [(grads.at[it, f], grads.at[it, f], peer) for peer in f_peers],
            grads.at[it, pl.ds(0, freq_size - 1)],
        )
        gradient = grads[it, 0]
        for j in range(1, freq_size):
            gradient = gradient + grads[it, j]
        gradient = (-2.0 * inverse) * gradient
        squares = gradient * gradient
        normed = squares[:, :mics]
        for k in range(1, points // mics):
            normed = normed + squares[:, k * mics : (k + 1) * mics]
        norms[it, far_id] = normed * (1.0 / freq_size)
        norm_copies = [(norms.at[it, far_id], norms.at[it, far_id], peer) for peer in far_peers]
        norm_like = norms.at[it, pl.ds(0, far_size - 1)]
        begin(base + 4, norm_copies, norm_like)

        mine = summed(2 * it + 1, base + 5, gradient) * inverse
        index = lax.broadcasted_iota(jnp.int32, (nb, rows, mics), 1) + chunk_id * rows
        column = lax.broadcasted_iota(jnp.int32, (nb, rows, mics), 2)
        curved = mine * mine * jnp.where(index == column, 1.0, 2.0)
        curved = jnp.sum(jnp.sum(curved, axis=0), axis=0, keepdims=True)
        finish(base + 4, norm_copies, norm_like)
        parts_a[it, core] = jnp.concatenate([jnp.sum(norms[it], axis=0), curved], axis=0)
        exchange(
            base + 7,
            [(parts_a.at[it, core], parts_a.at[it, core], other_core)],
            parts_a.at[it, 0],
        )
        own = x * chunks + chunk_id
        parts_b[it, own] = jnp.sum(parts_a[it], axis=0)
        exchange(
            base + 8,
            [(parts_b.at[it, own], parts_b.at[it, own], peer) for _, peer in clients_x],
            parts_b.at[it, pl.ds(0, cols_x * chunks - 1)],
        )
        sums = jnp.sum(jnp.sum(parts_b[it], axis=0), axis=1, keepdims=True)
        step_length = 0.5 * sums[0:1] / sums[1:2]
        updated = jnp.maximum(strength[...] - step_length * gradient, 0.0)
        if it < ITERS - 1:
            strength[...] = updated
        else:
            out_ref[...] = updated

    for phase, like in unsent:
        pltpu.make_async_copy(like, like, send_sem.at[phase]).wait()


def local(grid_size, freq_size, bin_index, microphones, grid_points, cross_spectra, initial_strengths):
    nb = bin_index.shape[0]
    mics = microphones.shape[1]
    points = grid_points.shape[1]
    ny = GRID_Y
    nz = grid_size // ny
    far_size = nz // NEAR
    chunks = ny * NEAR
    rows = mics // chunks
    hbm = pl.BlockSpec(memory_space=pltpu.HBM)
    out = pl.pallas_call(
        functools.partial(kernel, grid_size, freq_size),
        out_shape=jax.ShapeDtypeStruct((1, points), F32),
        in_specs=[hbm] * 5,
        out_specs=pl.BlockSpec(memory_space=pltpu.VMEM),
        scratch_shapes=[
            pltpu.SMEM((nb,), jnp.int32),
            pltpu.VMEM((3, mics), F32),
            pltpu.VMEM((3, points), F32),
            pltpu.VMEM((nb, 2, mics, mics), F32),
            pltpu.VMEM((1, points), F32),
            pltpu.VMEM((3, mics, mics), F32),
            pltpu.VMEM((nb, 2 * mics, points), BF16),
            pltpu.VMEM((nb, 2 * mics, 2 * mics), F32),
            pltpu.VMEM((2 * ITERS, chunks, nb, rows, mics), F32),
            pltpu.VMEM((2 * ITERS, chunks - 1, nb, rows, mics), F32),
            pltpu.VMEM((2 * ITERS, far_size, nb, rows, mics), F32),
            pltpu.VMEM((ITERS, chunks, nb, rows, mics), F32),
            pltpu.VMEM((ITERS, freq_size, 1, points), F32),
            pltpu.VMEM((ITERS, far_size, 1, mics), F32),
            pltpu.VMEM((ITERS, CORES, 2, mics), F32),
            pltpu.VMEM((ITERS, freq_size // CORES * chunks, 2, mics), F32),
            pltpu.SemaphoreType.DMA((5,)),
            pltpu.SemaphoreType.DMA((9 * ITERS,)),
            pltpu.SemaphoreType.DMA((9 * ITERS,)),
        ],
        compiler_params=pltpu.CompilerParams(
            collective_id=0, has_side_effects=True, vmem_limit_bytes=62 * 1024 * 1024
        ),
        name="map_fit",
    )(bin_index, microphones, grid_points, cross_spectra, initial_strengths.reshape(1, points))
    return out.reshape(points)


def solution(mesh):
    placed = (P("freq"), P(), P(None, "grid"), P("freq", None, None, None), P("grid"))
    body = functools.partial(local, mesh.shape["grid"], mesh.shape["freq"])
    return jax.shard_map(body, mesh=mesh, in_specs=placed, out_specs=P("grid"), check_vma=False)
```

```python
import functools
import math

import jax
import jax.numpy as jnp
from jax import lax
from jax.experimental import pallas as pl
from jax.experimental.pallas import tpu as pltpu
from jax.sharding import PartitionSpec as P

ITERS = 2
GRID_Y = 4
CORES = 2
HALVES = 2
PHASES = 16
NEAR = 4

HEIGHT = 2.5
REFERENCE_RANGE = 2.5
TURN_STEP = 25.0 / 343.0
HALF_PI = math.pi / 2.0

MESH = pl.DeviceIdType.MESH
F32 = jnp.float32
BF16 = jnp.bfloat16

SIN_COEFFS = (3.141590270, -5.167406733, 2.544010518, -0.559462455)
COS_COEFFS = (0.999993249, -4.933934668, 4.041248102, -1.222031763)


def horner(coeffs, u):
    value = coeffs[-1]
    for c in coeffs[-2::-1]:
        value = value * u + c
    return value


def kernel(
    grid_size,
    freq_size,
    bins_hbm,
    mics_hbm,
    points_hbm,
    cross_hbm,
    start_hbm,
    out_ref,
    bins_ref,
    mics_ref,
    points_ref,
    cross_ref,
    strength,
    mic_cols,
    steer,
    gram,
    scattered,
    arrived,
    far,
    gather,
    terms,
    grads,
    norms,
    parts_a,
    parts_b,
    load_sem,
    send_sem,
    recv_sem,
):
    nb = bins_ref.shape[0]
    mics = mics_ref.shape[1]
    points = points_ref.shape[1]
    ny = GRID_Y
    nz = grid_size // ny
    far_size = nz // NEAR
    chunks = ny * NEAR
    rows = mics // chunks
    total = points * grid_size
    inverse = 1.0 / total

    g = lax.axis_index("grid")
    f = lax.axis_index("freq")
    y, z = lax.div(g, nz), lax.rem(g, nz)
    cols_x = freq_size // CORES
    x, core = lax.div(f, CORES), lax.rem(f, CORES)
    chunk_id = y * NEAR + lax.rem(z, NEAR)
    far_id = lax.div(z, NEAR)

    def at(y_id, z_id, f_id):
        return {"grid": y_id * nz + z_id, "freq": f_id}

    def near(reach, x_reach=(0,)):
        steps = [
            (min(dx, cols_x - dx) + min(dy, ny - dy) + hops, dx, dy, dz)
            for dx in x_reach
            for dy in range(ny)
            for hops, dz in reach
        ]
        peers = []
        for hops, dx, dy, dz in sorted(steps, key=lambda step: -step[0]):
            if hops == 0:
                continue
            y_id = lax.rem(y + dy, ny)
            z_id = lax.rem(z + dz + nz, nz)
            f_id = lax.rem(x + dx, cols_x) * CORES + core
            peers.append((y_id * NEAR + lax.rem(z_id, NEAR), at(y_id, z_id, f_id)))
        return peers

    two = 2 - 4 * core
    owners = near(((0, 0), (1, 1), (1, -1), (2, two)))
    clients = near(((0, 0), (1, 1), (1, -1), (2, -two)))
    all_x = tuple(range(1, cols_x))
    clients_x = near(((0, 0), (1, 1), (1, -1), (2, -two)), (0,) + all_x)
    owners_x = near(((0, 0), (1, 1), (1, -1), (2, two)), all_x)
    neighbours = near(((0, 0), (1, 1), (1, -1), (2, 2), (2, -2)))
    far_peers = [at(y, lax.rem(z + d * NEAR, nz), f) for d in (2, 1, 3) if d < far_size]
    other_core = at(y, z, x * CORES + 1 - core)
    f_steps = [(dx, dc) for dx in (2, 1, 3) if dx < cols_x for dc in (1, 0)] + [(0, 1)]
    f_peers = [
        at(y, z, lax.rem(x + dx, cols_x) * CORES + lax.rem(core + dc, CORES)) for dx, dc in f_steps
    ]

    loads = [
        pltpu.make_async_copy(src, dst, load_sem.at[i])
        for i, (src, dst) in enumerate(
            (
                (bins_hbm, bins_ref),
                (mics_hbm, mics_ref),
                (points_hbm, points_ref),
                (start_hbm, strength),
                (cross_hbm, cross_ref),
            )
        )
    ]
    for load in loads:
        load.start()

    greeted = [peer for _, peer in neighbours] + far_peers + f_peers + [peer for _, peer in owners_x]
    barrier = pltpu.get_barrier_semaphore()
    for peer in greeted:
        pl.semaphore_signal(barrier, inc=1, device_id=peer, device_id_type=MESH)

    unsent = []

    def begin(phase, copies, like):
        for src, dst, peer in copies:
            pltpu.make_async_remote_copy(
                src_ref=src,
                dst_ref=dst,
                send_sem=send_sem.at[phase],
                recv_sem=recv_sem.at[phase],
                device_id=peer,
                device_id_type=MESH,
            ).start()
        if copies:
            unsent.append((phase, like))

    def finish(phase, copies, like):
        if copies:
            pltpu.make_async_copy(like, like, recv_sem.at[phase]).wait()

    def exchange(phase, copies, like):
        begin(phase, copies, like)
        finish(phase, copies, like)

    for load in loads[:3]:
        load.wait()

    for axis in range(3):
        mic_cols[axis] = jnp.transpose(jnp.broadcast_to(mics_ref[axis : axis + 1, :], (mics, mics)))
    scale = [bins_ref[b].astype(F32) * TURN_STEP for b in range(nb)]
    sub, lanes = 16, 512
    blocks_m = mics // sub

    def steer_block(i, carry):
        m0 = pl.multiple_of(lax.rem(i, blocks_m) * sub, sub)
        c0 = pl.multiple_of(lax.div(i, blocks_m) * lanes, lanes)
        cols = pl.ds(c0, lanes)

        def mic(axis):
            tile = mic_cols[axis, pl.ds(m0, sub), :]
            return jnp.concatenate([tile] * (lanes // mics), axis=1)

        dx = points_ref[0:1, cols] - mic(0)
        dy = points_ref[1:2, cols] - mic(1)
        dz = (points_ref[2:3, cols] + HEIGHT) - mic(2)
        square = dx * dx + dy * dy + dz * dz
        inv = lax.rsqrt(square)
        inv = inv * (1.5 - 0.5 * square * inv * inv)
        distance = square * inv
        amplitude = REFERENCE_RANGE * inv
        for b in range(nb):
            turns = distance * scale[b]
            frac = turns - jnp.round(turns)
            u = frac * frac
            half_sin = frac * horner(SIN_COEFFS, u)
            half_cos = horner(COS_COEFFS, u)
            twice = (2.0 * amplitude) * half_sin
            real = amplitude - twice * half_sin
            imag = -(twice * half_cos)
            steer[b, pl.ds(m0, sub), cols] = real.astype(BF16)
            steer[b, pl.ds(m0 + mics, sub), cols] = imag.astype(BF16)
        return carry

    lax.fori_loop(0, blocks_m * (points // lanes), steer_block, 0)

    row = lax.broadcasted_iota(jnp.int32, (mics, mics), 0)
    col = lax.broadcasted_iota(jnp.int32, (mics, mics), 1)
    upper = row <= col
    diagonal = row == col

    def product(b, cols, weights):
        s = steer[b, :, cols]
        return lax.dot_general(
            (s.astype(F32) * weights).astype(BF16),
            s,
            (((1,), (1,)), ((), ())),
            preferred_element_type=F32,
        )

    def scatter(slot, b, phase):
        real = gram[b, :mics, :mics] + gram[b, mics:, mics:]
        imag = gram[b, mics:, :mics] - gram[b, :mics, mics:]
        scattered[slot, b] = jnp.where(upper, real, imag).reshape(chunks, rows, mics)
        begin(
            phase,
            [
                (scattered.at[slot, b, k], arrived.at[slot, b, i], peer)
                for i, (k, peer) in enumerate(owners)
            ],
            arrived.at[slot, b],
        )

    def swap(slot, b, phase):
        finish(phase, owners, arrived.at[slot, b])
        far[slot, b, far_id] = scattered[slot, b, chunk_id] + jnp.sum(arrived[slot, b], axis=0)
        mine = far.at[slot, b, far_id]
        begin(phase + nb, [(mine, mine, peer) for peer in far_peers], far.at[slot, b, pl.ds(0, far_size - 1)])

    def summed(slot, b, phase):
        finish(phase + nb, far_peers, far.at[slot, b, pl.ds(0, far_size - 1)])
        return jnp.sum(far[slot, b], axis=0)

    bins = range(nb)
    half = points // HALVES
    halves = [pl.ds(h * half, half) for h in range(HALVES)]
    width = 512
    index = lax.broadcasted_iota(jnp.int32, (rows, mics), 0) + chunk_id * rows
    column = lax.broadcasted_iota(jnp.int32, (rows, mics), 1)
    twice = jnp.where(index == column, 1.0, 2.0)

    for it in range(ITERS):
        base = PHASES * it
        model_phase = base
        gather_phase = model_phase + 2 * nb
        gradient_phase = gather_phase + nb
        norm_phase = gradient_phase + HALVES
        direction_phase = norm_phase + 1
        core_phase = direction_phase + 2 * nb

        if it == 0:
            loads[3].wait()
        for b in bins:
            gram[b] = product(b, slice(None), strength[...])
            if it == 0 and b == 0:
                pl.semaphore_wait(barrier, len(greeted))
            scatter(2 * it, b, model_phase + b)
        for b in bins:
            swap(2 * it, b, model_phase + b)
        for b in bins:
            gather[it, b, chunk_id] = summed(2 * it, b, model_phase + b)
            mine = gather.at[it, b, chunk_id]
            begin(
                gather_phase + b,
                [(mine, mine, peer) for _, peer in clients],
                gather.at[it, b, pl.ds(0, chunks - 1)],
            )
        if it == 0:
            loads[4].wait()

        for b in bins:
            finish(gather_phase + b, clients, gather.at[it, b, pl.ds(0, chunks - 1)])
            model = gather[it, b].reshape(mics, mics)
            flipped = jnp.transpose(model)
            model_real = jnp.where(upper, model, flipped)
            model_imag = jnp.where(diagonal, 0.0, jnp.where(upper, -flipped, model))
            res_real = cross_ref[b, 0] - model_real * inverse
            res_imag = cross_ref[b, 1] - model_imag * inverse
            operator = jnp.concatenate(
                [
                    jnp.concatenate([res_real, -res_imag], axis=1),
                    jnp.concatenate([res_imag, res_real], axis=1),
                ],
                axis=0,
            ).astype(BF16)
            for k in range(points // width):
                cols = pl.ds(k * width, width)
                s = steer[b, :, cols]
                applied = jnp.dot(operator, s, preferred_element_type=F32)
                term = (s.astype(F32) * applied).reshape(2 * mics // 8, 8, width)
                term = jnp.sum(term, axis=0)
                if b > 0:
                    term = term + terms[:, cols]
                if b < nb - 1:
                    terms[:, cols] = term
                    continue
                h, offset = k * width // half, k * width % half
                grads[it, h, f, :, pl.ds(offset, width)] = jnp.sum(term, axis=0, keepdims=True)
                if offset + width == half:
                    mine = grads.at[it, h, f]
                    begin(
                        gradient_phase + h,
                        [(mine, mine, peer) for peer in f_peers],
                        grads.at[it, h, pl.ds(0, freq_size - 1)],
                    )

        parts = []
        for h in range(HALVES):
            finish(gradient_phase + h, f_peers, grads.at[it, h, pl.ds(0, freq_size - 1)])
            part = grads[it, h, 0]
            for j in range(1, freq_size):
                part = part + grads[it, h, j]
            part = (-2.0 * inverse) * part
            parts.append(part)
            for b in bins:
                if h == 0:
                    gram[b] = product(b, halves[h], part)
                else:
                    gram[b] += product(b, halves[h], part)
                if h == HALVES - 1:
                    scatter(2 * it + 1, b, direction_phase + b)
        normed = None
        for part in parts:
            squares = part * part
            for k in range(half // mics):
                piece = squares[:, k * mics : (k + 1) * mics]
                normed = piece if normed is None else normed + piece
        norms[it, far_id] = normed * (1.0 / freq_size)
        norm_copies = [(norms.at[it, far_id], norms.at[it, far_id], peer) for peer in far_peers]
        norm_like = norms.at[it, pl.ds(0, far_size - 1)]
        begin(norm_phase, norm_copies, norm_like)

        for b in bins:
            swap(2 * it + 1, b, direction_phase + b)
        finish(norm_phase, norm_copies, norm_like)
        norm_part = jnp.sum(norms[it], axis=0)
        curved = None
        for b in bins:
            mine = summed(2 * it + 1, b, direction_phase + b) * inverse
            mine = mine * mine * twice
            curved = mine if curved is None else curved + mine
        curved = jnp.sum(curved, axis=0, keepdims=True)
        parts_a[it, core] = jnp.concatenate([norm_part, curved], axis=0)
        exchange(
            core_phase,
            [(parts_a.at[it, core], parts_a.at[it, core], other_core)],
            parts_a.at[it, 0],
        )
        own = x * chunks + chunk_id
        parts_b[it, own] = jnp.sum(parts_a[it], axis=0)
        exchange(
            core_phase + 1,
            [(parts_b.at[it, own], parts_b.at[it, own], peer) for _, peer in clients_x],
            parts_b.at[it, pl.ds(0, cols_x * chunks - 1)],
        )
        sums = jnp.sum(jnp.sum(parts_b[it], axis=0), axis=1, keepdims=True)
        step_length = 0.5 * sums[0:1] / sums[1:2]
        for h in range(HALVES):
            updated = jnp.maximum(strength[:, halves[h]] - step_length * parts[h], 0.0)
            if it < ITERS - 1:
                strength[:, halves[h]] = updated
            else:
                out_ref[:, halves[h]] = updated

    for phase, like in unsent:
        pltpu.make_async_copy(like, like, send_sem.at[phase]).wait()


def local(grid_size, freq_size, bin_index, microphones, grid_points, cross_spectra, initial_strengths):
    nb = bin_index.shape[0]
    mics = microphones.shape[1]
    points = grid_points.shape[1]
    ny = GRID_Y
    nz = grid_size // ny
    far_size = nz // NEAR
    chunks = ny * NEAR
    rows = mics // chunks
    start = initial_strengths.reshape(1, points)
    arguments = (bin_index, microphones, grid_points, cross_spectra, start)
    hbm = pl.BlockSpec(memory_space=pltpu.HBM)
    out = pl.pallas_call(
        functools.partial(kernel, grid_size, freq_size),
        out_shape=jax.ShapeDtypeStruct((1, points), F32),
        in_specs=[hbm] * 5,
        out_specs=pl.BlockSpec(memory_space=pltpu.VMEM),
        scratch_shapes=[
            pltpu.SMEM((nb,), jnp.int32),
            pltpu.VMEM((3, mics), F32),
            pltpu.VMEM((3, points), F32),
            pltpu.VMEM((nb, 2, mics, mics), F32),
            pltpu.VMEM((1, points), F32),
            pltpu.VMEM((3, mics, mics), F32),
            pltpu.VMEM((nb, 2 * mics, points), BF16),
            pltpu.VMEM((nb, 2 * mics, 2 * mics), F32),
            pltpu.VMEM((2 * ITERS, nb, chunks, rows, mics), F32),
            pltpu.VMEM((2 * ITERS, nb, chunks - 1, rows, mics), F32),
            pltpu.VMEM((2 * ITERS, nb, far_size, rows, mics), F32),
            pltpu.VMEM((ITERS, nb, chunks, rows, mics), F32),
            pltpu.VMEM((8, points), F32),
            pltpu.VMEM((ITERS, HALVES, freq_size, 1, points // HALVES), F32),
            pltpu.VMEM((ITERS, far_size, 1, mics), F32),
            pltpu.VMEM((ITERS, CORES, 2, mics), F32),
            pltpu.VMEM((ITERS, freq_size // CORES * chunks, 2, mics), F32),
            pltpu.SemaphoreType.DMA((5,)),
            pltpu.SemaphoreType.DMA((PHASES * ITERS,)),
            pltpu.SemaphoreType.DMA((PHASES * ITERS,)),
        ],
        compiler_params=pltpu.CompilerParams(
            collective_id=0, has_side_effects=True, vmem_limit_bytes=48 * 1024 * 1024
        ),
        name="map_fit",
    )(*(pltpu.with_memory_space_constraint(a, pltpu.HBM) for a in arguments))
    return out.reshape(points)


def solution(mesh):
    placed = (P("freq"), P(), P(None, "grid"), P("freq", None, None, None), P("grid"))
    body = functools.partial(local, mesh.shape["grid"], mesh.shape["freq"])
    return jax.shard_map(body, mesh=mesh, in_specs=placed, out_specs=P("grid"), check_vma=False)
```
